128 devices in a mesh: row: 8 (over x, core), col: 16 (over y, z).
Axes of the slice: x: 4, y: 4, z: 4, core: 2. Of those that a mesh axis runs over, the one named last changes fastest.
Arguments:
- left_tiles: bfloat16 [8192, 4096], P('row', 'col'), may hold values from -6 to 6
- right_tiles: bfloat16 [4096, 16384], P('row', 'col'), may hold values from -0.09375 to 0.09375
- left_mask: int32 [64, 32], P('row', 'col'), may hold values from 0 to 1, as said below
- right_mask: int32 [32, 128], P('row', 'col'), may hold values from 0 to 1, as said below
- cycle_weight: bfloat16 [16384, 1024], P('col', 'row'), may hold values from -0.046875 to 0.046875
Outputs:
- cycle_out: float32 [64, 128, 1024], P('row', 'col')
The draws below stay inside these ranges and needn't reach their ends.
Inputs may be any that keep to these rules, and one draw needn't show every extreme that they name: `left_mask`: each tile row i keeps each of its tiles with chance one, two or three thirds, the level drawn per row. `right_mask`: each tile column a keeps each of its tiles with chance one, two or three thirds, the level drawn per column.
All inputs are finite; a program needn't handle non-finite values.
Results may differ from the reference program's by a relative error of at most 0.0029.
Values may be sent and summed in bfloat16 or wider, within the bound.
A program may use at most 64 MiB of HBM per device.

```python
import jax
import jax.numpy as jnp

TILE = 128
JOCC = 128
VIRT_B = 128
OCC = 64
VA = 128
KTILES = 32
KC = 1024


def draw_left_mask(key, part):
    key = jax.random.fold_in(key, 11)
    first, second = jax.random.split(key)
    level = jax.random.randint(first, (OCC, 1), 1, 4)
    coin = jax.random.randint(second, (OCC, KTILES), 0, 3)
    return (coin < level).astype(jnp.int32)


def draw_right_mask(key, part):
    key = jax.random.fold_in(key, 23)
    first, second = jax.random.split(key)
    level = jax.random.randint(first, (1, VA), 1, 4)
    coin = jax.random.randint(second, (KTILES, VA), 0, 3)
    return (coin < level).astype(jnp.int32)


def levels(key, dims, shards, least, largest):
    def one(axis_at, parts):
        steps = jax.random.uniform(jax.random.fold_in(jax.random.fold_in(key, 6), axis_at), (parts,), jnp.float32, least / len(shards), largest / len(shards))
        return jnp.repeat(jnp.exp(steps), dims[axis_at] // parts).reshape((-1,) + (1,) * (len(dims) - axis_at - 1))

    loudness = one(*shards[0])
    for cut in shards[1:]:
        loudness = loudness * one(*cut)
    return loudness


def noise(key, dims, spread, bound, cuts=(), kind=jnp.bfloat16):
    result = jax.random.normal(key, dims, jnp.float32) * spread
    if len(cuts) > 0:
        result = levels(key, dims, cuts, -0.22, 0.18) * result
    return jnp.clip(result, min=-bound, max=bound).astype(kind)


def setup_inputs(seed: int = 0) -> dict:
    keys = jax.random.split(jax.random.key(seed), 6)
    return {
        "left_tiles": noise(keys[0], (OCC * JOCC, KTILES * TILE), 1.0, 6.0, ((0, 8), (1, 16))),
        "right_tiles": noise(keys[1], (KTILES * TILE, VA * VIRT_B), (KTILES * TILE) ** -0.5, 0.09375, ((0, 8), (1, 16))),
        "left_mask": draw_left_mask(jax.random.fold_in(keys[5], 71), 0),
        "right_mask": draw_right_mask(jax.random.fold_in(keys[5], 71), 0),
        "cycle_weight": noise(keys[4], (JOCC * VIRT_B, KC), (JOCC * VIRT_B) ** -0.5, 0.046875, ((0, 16), (1, 8))),
    }


def apply_mask(tiles, mask):
    rows, cols = tiles.shape
    mrows, mcols = mask.shape
    shaped = tiles.reshape(mrows, rows // mrows, mcols, cols // mcols)
    return (shaped * mask[:, None, :, None].astype(tiles.dtype)).reshape(rows, cols)


def reference(left_tiles, right_tiles, left_mask, right_mask, cycle_weight):
    masked_left = apply_mask(left_tiles, left_mask)
    masked_right = apply_mask(right_tiles, right_mask)
    pair_block = jnp.dot(masked_left, masked_right, preferred_element_type=jnp.float32).astype(jnp.bfloat16)
    relaid = pair_block.reshape(OCC, JOCC, VA, VIRT_B).astype(jnp.float32)
    operand = cycle_weight.reshape(JOCC, VIRT_B, KC).astype(jnp.float32)
    return jnp.einsum('ijab,jbk->iak', relaid, operand)
```

```python
import jax
import jax.numpy as jnp
from jax import lax
from jax.experimental import pallas as pl
from jax.experimental.pallas import tpu as pltpu
from jax.sharding import PartitionSpec as P

MESH = pl.DeviceIdType.MESH
F32 = jnp.float32
BF16 = jnp.bfloat16

GROUPS = (0, 2, -1, 1)
ITEMS = (("L", 0), ("L", 1), ("W", 0), ("W", 1), ("L", 2), ("L", 3))
LAG = 3
STAGES = 7


def norm(d):
    return (d + 1) % 4 - 1


def kernel(l_ref, r_ref, w_ref, lm_ref, rm_ref, out_ref,
           L, R, W, lf, lp, acc, lhs, part, sib, far,
           g_send, g_recv, a_send, a_recv, r_send, r_recv, s_send, s_recv, o_send, o_recv):
    row, col = lax.axis_index("row"), lax.axis_index("col")
    x, core = row // 2, row % 2
    y, z = col // 4, col % 4
    sent = []

    def row_at(dx, e):
        other = core if e == 0 else 1 - core
        return ((x + dx + 4) % 4) * 2 + other

    def col_at(dy, dz):
        return ((y + dy + 4) % 4) * 4 + (z + dz + 4) % 4

    def put(src, dst, send, recv, device):
        copy = pltpu.make_async_remote_copy(
            src_ref=src, dst_ref=dst, send_sem=send, recv_sem=recv,
            device_id=device, device_id_type=MESH)
        copy.start()
        sent.append(copy)

    def arrived(dst, send, recv):
        pltpu.make_async_remote_copy(
            src_ref=dst, dst_ref=dst, send_sem=send, recv_sem=recv,
            device_id=(row_at(0, 1), col), device_id_type=MESH).wait_recv()

    barrier = pltpu.get_barrier_semaphore()
    peers = [(row, col_at(1, 0)), (row, col_at(-1, 0)), (row, col_at(0, 1)), (row, col_at(0, -1))]
    peers += [(row_at(dx, e), col) for dx in GROUPS for e in (0, 1) if (dx, e) != (0, 0)]
    for peer in peers:
        pl.semaphore_signal(barrier, inc=1, device_id=peer, device_id_type=MESH)

    for i in range(8):
        for t in range(2):
            keep = lm_ref[i, t].astype(F32)
            lf[t, i * 128:(i + 1) * 128, :] = l_ref[i * 128:(i + 1) * 128, t * 128:(t + 1) * 128].astype(F32) * keep
    for r in range(8):
        for t in range(2):
            for q in range(0, 16, 2):
                pair = [lf[t, pl.ds(8 * (q + s) + r, 8, stride=128), :] for s in (0, 1)]
                lp[r, q * 8:q * 8 + 16, t * 128:(t + 1) * 128] = jnp.concatenate(pair, axis=0).astype(BF16)
    for t in range(4):
        here = pl.ds(pl.multiple_of(row * 512 + t * 128, 128), 128)
        for a in range(8):
            keep = rm_ref[t, a].astype(F32)
            R[here, a * 128:(a + 1) * 128] = (r_ref[t * 128:(t + 1) * 128, a * 128:(a + 1) * 128].astype(F32) * keep).astype(BF16)
    own_l = pl.ds(pl.multiple_of(col * 256, 256), 256)
    own_w = pl.ds(pl.multiple_of(col * 128, 128), 128)
    row_w = pl.ds(pl.multiple_of(row * 128, 128), 128)
    L[0, :, own_l] = lp[row]
    W[own_w, row_w] = w_ref[row_w, :]

    pl.semaphore_wait(barrier, len(peers))

    def exchange_l(g, e):
        dx = GROUPS[g]
        slot = 2 * GROUPS.index(norm(-dx)) + e
        to = row_at(dx, e)
        put(lp.at[to], L.at[slot, :, own_l], a_send.at[0, 2 * g + e], a_recv.at[0, slot], (to, col))

    def exchange_w(g, e):
        dx = GROUPS[g]
        slot = 2 * GROUPS.index(norm(-dx)) + e
        to = row_at(dx, e)
        put(w_ref.at[pl.ds(pl.multiple_of(to * 128, 128), 128), :], W.at[own_w, row_w],
            a_send.at[1, 2 * g + e], a_recv.at[1, slot], (to, col))

    def exchanged_l(slot):
        arrived(L.at[slot, :, own_l], a_send.at[0, slot], a_recv.at[0, slot])

    def exchanged_w(slot):
        g, e = slot // 2, slot % 2
        lanes = pl.ds(pl.multiple_of(row_at(GROUPS[g], e) * 128, 128), 128)
        arrived(W.at[own_w, lanes], a_send.at[1, slot], a_recv.at[1, slot])

    def r_piece(dx, e, p):
        return R.at[pl.ds(pl.multiple_of(row_at(dx, e) * 512 + p * 128, 128), 128), :]

    r_count = [0]

    def r_put(dx, p, to):
        view = r_piece(dx, 0, p)
        if to is None:
            recv, device = s_recv.at[GROUPS.index(dx), p], (row_at(0, 1), col)
        else:
            recv, device = r_recv.at[GROUPS.index(norm(dx - to)), p], (row_at(to, 0), col)
        put(view, view, r_send.at[r_count[0]], recv, device)
        r_count[0] += 1

    def r_arrived(dx, p):
        arrived(r_piece(dx, 0, p), r_send.at[0], r_recv.at[GROUPS.index(dx), p])

    def r_stage0(p):
        r_put(0, p, 1)
        r_put(0, p, -1)
        r_put(0, p, None)

    def r_stage1(p):
        r_arrived(-1, p)
        if p < 2:
            r_put(-1, p, 1)
        r_put(-1, p, None)
        r_arrived(1, p)
        if p >= 2:
            r_put(1, p, -1)
        r_put(1, p, None)

    def r_stage2(p):
        r_arrived(2, p)
        r_put(2, p, None)

    def r_stage3():
        for dx in GROUPS:
            for p in range(4):
                arrived(r_piece(dx, 1, p), s_send, s_recv.at[GROUPS.index(dx), p])

    def block(n, h, at):
        kind, g = ITEMS[n]
        if kind == "L":
            return L.at[2 * g + h, :, pl.ds(pl.multiple_of(at * 256, 256), 256)]
        return W.at[pl.ds(pl.multiple_of(at * 128 + (2 * g + h) * 32, 32), 32), :]

    def along(h, p, q):
        return col_at(p, q) if h == 0 else col_at(q, p)

    def sem_of(p, q):
        return 4 * (p % 4) + q % 4

    counts = {}

    def g_put(n, h, p, q, ep, eq):
        view = block(n, h, along(h, p, q))
        k = counts.get((n, h), 0)
        counts[n, h] = k + 1
        put(view, view, g_send.at[n, h, k], g_recv.at[n, h, sem_of(p - ep, q - eq)], (row, along(h, ep, eq)))

    def g_arrived(n, h, p, q):
        arrived(block(n, h, along(h, p, q)), g_send.at[n, h, 0], g_recv.at[n, h, sem_of(p, q)])

    def stage(n, k):
        if k == 0:
            kind, g = ITEMS[n]
            if kind == "W" and g == 0:
                for slot in range(1, 8):
                    exchanged_w(slot)
        for h in (0, 1):
            if k == 0:
                if kind == "L" and 2 * g + h > 0:
                    exchanged_l(2 * g + h)
                for e in (1, -1):
                    g_put(n, h, 0, 0, e, 0)
                    g_put(n, h, 0, 0, 0, e)
            elif k == 1:
                way = 1 if n % 2 == 0 else -1
                for d in (-1, 1):
                    g_arrived(n, h, d, 0)
                    if d == -way:
                        g_put(n, h, d, 0, way, 0)
                    for e in (1, -1):
                        g_put(n, h, d, 0, 0, e)
            elif k == 2:
                g_arrived(n, h, 0, -1)
                g_put(n, h, 0, -1, 0, 1)
                g_arrived(n, h, 0, 1)
            elif k == 3:
                g_arrived(n, h, 2, 0)
                for e in (1, -1):
                    g_put(n, h, 2, 0, 0, e)
            elif k == 4:
                for d in (-1, 1):
                    g_arrived(n, h, d, 1)
                    g_put(n, h, d, 1, 0, -1)
                    g_arrived(n, h, d, -1)
            elif k == 5:
                g_arrived(n, h, 2, -1)
                g_put(n, h, 2, -1, 0, 1)
                g_arrived(n, h, 2, 1)
            else:
                for d in (0, -1, 1, 2):
                    g_arrived(n, h, d, 2)

    def multiply(g):
        @pl.loop(0, 4)
        def _(n):
            lanes = pl.ds(pl.multiple_of(n * 256, 256), 256)
            acc[:, lanes] = jnp.dot(L[2 * g:2 * g + 2].reshape(256, 4096), R[:, lanes], preferred_element_type=F32)

    def contract(g):
        for q in range(16):
            for a in range(8):
                both = [acc[e * 128 + q * 8:e * 128 + q * 8 + 8, a * 128:(a + 1) * 128] for e in (0, 1)]
                lhs[a * 16:(a + 1) * 16, q * 128:(q + 1) * 128] = jnp.concatenate(both, axis=0).astype(BF16)

        @pl.loop(0, 4)
        def _(n):
            lanes = pl.ds(pl.multiple_of(n * 256, 256), 256)
            share = jnp.dot(lhs[...], W[:, lanes], preferred_element_type=F32)
            part[g, :, :, :, lanes] = share.reshape(8, 2, 8, 256)
        put(part.at[g, :, 1], sib.at[g], o_send.at[0, g], o_recv.at[0, g], (row_at(0, 1), col))

    def reduce(g):
        arrived(sib.at[g], o_send.at[0, g], o_recv.at[0, g])
        part[g, :, 0] = part[g, :, 0] + sib[g]
        if g > 0:
            put(part.at[g, :, 0], far.at[g - 1], o_send.at[1, g], o_recv.at[1, g], (row_at(GROUPS[g], 0), col))

    extra = {
        1: [lambda: r_stage1(0)], 3: [lambda: r_stage1(1)],
        5: [lambda: r_stage1(2)], 7: [lambda: r_stage1(3)],
        9: [lambda: r_stage2(0)], 10: [lambda: r_stage2(1)],
        11: [lambda: r_stage2(2)], 12: [lambda: r_stage2(3)],
        14: [r_stage3, lambda: multiply(0)],
        15: [lambda: contract(0)],
        17: [lambda: multiply(1), lambda: contract(1)],
        18: [lambda: reduce(0), lambda: reduce(1)],
        19: [lambda: multiply(2), lambda: contract(2)],
        20: [lambda: reduce(2)],
    }
    exchange_l(0, 1)
    exchange_l(1, 0)
    exchange_l(1, 1)
    r_stage0(0)
    for g in range(4):
        for e in (0, 1):
            if (g, e) != (0, 0):
                exchange_w(g, e)
    r_stage0(1)
    r_stage0(2)
    r_stage0(3)
    for g in (2, 3):
        for e in (0, 1):
            exchange_l(g, e)
    last = LAG * (len(ITEMS) - 1) + STAGES
    for tau in range(last):
        for n in range(len(ITEMS)):
            k = tau - LAG * n
            if 0 <= k < STAGES:
                stage(n, k)
        for do in extra.get(tau, ()):
            do()
    multiply(3)
    contract(3)
    reduce(3)
    for g in range(1, 4):
        arrived(far.at[g - 1], o_send.at[1, g], o_recv.at[1, g])
    out_ref[...] = part[0, :, 0] + far[0] + far[1] + far[2]
    for copy in sent:
        copy.wait_send()


def body(left_tiles, right_tiles, left_mask, right_mask, cycle_weight):
    vmem = pl.BlockSpec(memory_space=pltpu.VMEM)
    smem = pl.BlockSpec(memory_space=pltpu.SMEM)
    dma = pltpu.SemaphoreType.DMA
    total = pl.pallas_call(
        kernel,
        out_shape=jax.ShapeDtypeStruct((8, 8, 1024), F32),
        in_specs=[vmem, vmem, vmem, smem, smem],
        out_specs=vmem,
        scratch_shapes=[
            pltpu.VMEM((8, 128, 4096), BF16),
            pltpu.VMEM((4096, 1024), BF16),
            pltpu.VMEM((2048, 1024), BF16),
            pltpu.VMEM((2, 1024, 128), F32),
            pltpu.VMEM((8, 128, 256), BF16),
            pltpu.VMEM((256, 1024), F32),
            pltpu.VMEM((128, 2048), BF16),
            pltpu.VMEM((4, 8, 2, 8, 1024), F32),
            pltpu.VMEM((4, 8, 8, 1024), F32),
            pltpu.VMEM((3, 8, 8, 1024), F32),
            dma((len(ITEMS), 2, 15)),
            dma((len(ITEMS), 2, 16)),
            dma((2, 8)),
            dma((2, 8)),
            dma((28,)),
            dma((4, 4)),
            dma,
            dma((4, 4)),
            dma((2, 4)),
            dma((2, 4)),
        ],
        compiler_params=pltpu.CompilerParams(
            collective_id=0, has_side_effects=True, vmem_limit_bytes=56 * 1024 * 1024),
        cost_estimate=pl.CostEstimate(flops=11 * 10**9, bytes_accessed=4 * 2**20, transcendentals=0),
    )(left_tiles, right_tiles, cycle_weight, left_mask, right_mask)
    return jnp.swapaxes(total, 0, 1)


def solution(mesh):
    placed = (P("row", "col"), P("row", "col"), P("row", "col"), P("row", "col"), P("col", "row"))
    return jax.shard_map(
        body, mesh=mesh, in_specs=placed, out_specs=P("row", "col", None), check_vma=False
    )
```

```python
import jax
import jax.numpy as jnp
from jax import lax
from jax.experimental import pallas as pl
from jax.experimental.pallas import tpu as pltpu
from jax.sharding import PartitionSpec as P

MESH = pl.DeviceIdType.MESH
F32 = jnp.float32
BF16 = jnp.bfloat16

GROUPS = (0, 2, -1, 1)
ITEMS = (("S", 0), ("L", 1), ("W", 0), ("W", 1), ("L", 2), ("L", 3), ("S", 1))
GROUP_ITEMS = tuple(tuple(n for n, (kind, m) in enumerate(ITEMS) if (kind, m) in (("L", g), ("S", 2 * g), ("S", 2 * g + 1))) for g in range(4))
W_ITEMS = tuple(n for n, (kind, _) in enumerate(ITEMS) if kind == "W")


RATE = 42000.0
NEAR_RATE = 300000.0
LATENCY = 4.0
NEAR_LATENCY = 1.0
BACKLOG = 10.0
DEPTH = 7


NEAR = tuple((dy, dz) for dy in (-1, 0, 1) for dz in (-1, 0, 1))
FAR = tuple((dy, dz) for dy in (-1, 0, 1, 2) for dz in (-1, 0, 1, 2) if 2 in (dy, dz))


def norm(d):
    return (d + 1) % 4 - 1


def opposite(h, p, q):
    return ("y" if (p != 0) == (h == 0) else "z", p + q)


def tasks_of():
    tasks = {}
    for n, (kind, g) in enumerate(ITEMS):
        size = 32768 if kind == "S" else 65536
        for h in (0, 1):
            way = 1 if n % 2 == 0 else -1

            def go(p, q, ep, eq):
                return (("g", n, h, norm(p - ep), norm(q - eq)), opposite(h, ep, eq), size)

            if kind == "W":
                needs = [("w", m) for m in range(1, 8)]
            elif kind == "S":
                needs = [("l", g)] if g else []
            else:
                needs = [("l", 2 * g + h)]
            sends = [go(0, 0, e, 0) for e in (1, -1)] + [go(0, 0, 0, e) for e in (1, -1)]
            before = [("start", n, 0)] if h else [("start", n - 1, 1)] if n else []
            if n >= DEPTH:
                before = before + [("got", n - DEPTH, m, 2, 2) for m in (0, 1)]
            tasks["start", n, h] = (needs, [("prep",)] + before, 0.15, sends, 5)
            for p in range(-1, 3):
                for q in range(-1, 3):
                    if (p, q) == (0, 0):
                        continue
                    sends = []
                    if q == 0:
                        if p == -way:
                            sends.append(go(p, 0, way, 0))
                        sends += [go(p, 0, 0, e) for e in (1, -1)]
                    elif q == -1 and p in (0, 2):
                        sends.append(go(p, q, 0, 1))
                    elif q == 1 and p in (-1, 1):
                        sends.append(go(p, q, 0, -1))
                    tasks["got", n, h, p, q] = ([("g", n, h, p, q)], [("start", n, h)], 0.05 * (1 + len(sends)), sends, 10 + n)
    for p in range(4):
        sends = [(("r", -1, p), ("x", 1), 262144), (("r", 1, p), ("x", -1), 262144), (("s", 0, p), ("near", 0), 262144)]
        tasks["rstart", p] = ([], [("prep",)] + [("rstart", m) for m in range(p)], 0.5, sends, 40 + p)
        for d in (-1, 1):
            sends = [(("s", d, p), ("near", 0), 262144)]
            if (p < 2) == (d == -1):
                sends.append((("r", 2, p), ("x", -d), 262144))
            tasks["rgot", d, p] = ([("r", d, p)], [("rstart", p)], 0.1, sends, 20)
        tasks["rgot", 2, p] = ([("r", 2, p)], [("rstart", p)], 0.1, [(("s", 2, p), ("near", 0), 262144)], 20)
    tasks["rall",] = ([("s", d, p) for d in GROUPS for p in range(4)], [("rgot", d, p) for d in (-1, 1, 2) for p in range(4)], 0.1, [], 25)
    far = {-1: ("x", -1), 1: ("x", 1), 2: ("xx", 0)}
    for g in range(4):
        for e in (0, 1):
            slot = 2 * g + e
            if slot == 0:
                continue
            link = far.get(GROUPS[g], ("near", 0))
            tasks["lswap", g, e] = ([], [("prep",)], 0.05, [(("l", slot), link, 65536)], (30 if g in (0, 1) else 47))
            tasks["wswap", g, e] = ([], [("prep",)], 0.05, [(("w", slot), link, 32768)], 41)
    tasks["prep",] = ([], [], 2.0, [], 0)

    def arrived(items, halves=(0, 1)):
        return [(k, n, h, p, q) for n in items for h in halves for p in range(-1, 3) for q in range(-1, 3)
                for k in ("got",) if (p, q) != (0, 0)]

    def near(items):
        return [name for name in arrived(items) if 2 not in name[3:]]

    weights = arrived(W_ITEMS)
    for g in (1, 2, 3):
        for t in range(4):
            if g == 3:
                tasks["mul", g, t] = ([], [("rall",)] + near(GROUP_ITEMS[g]), 0.6, [], 60 + g)
                tasks["add", g, t] = ([], [("mul", g, t)] + arrived(GROUP_ITEMS[g]), 0.45, [], 60 + g)
            else:
                tasks["mul", g, t] = ([], [("rall",)] + arrived(GROUP_ITEMS[g]), 0.8, [], 60 + g)
        tasks["lhs", g] = ([], [("add" if g == 3 else "mul", g, t) for t in range(4)] + weights, 0.5, [], 60 + g)
        for u in (0, 1):
            tasks["con", g, u] = ([], [("lhs", g)] + [("con", g, 0)] * u, 0.6, [(("p", g, u), ("near", 0), 131072)], 55)
            tasks["red", g, u] = ([("p", g, u)], [("con", g, u)], 0.2, [(("f", g, u), far[GROUPS[g]], 65536)], 15)
            tasks["far", g, u] = ([("f", g, u)], [("red", g, u)], 0.1, [], 70)
    for e, n in enumerate(GROUP_ITEMS[0]):
        for t in range(4):
            tasks["blk", e, t] = ([], [("rall",)] + (near((n,)) if e else arrived((n,))), 0.4 if e else 0.6, [], 65)
            if e:
                tasks["bl2", e, t] = ([], [("blk", e, t)] + arrived((n,)), 0.35, [], 65)
    tasks["lhs", 0] = ([], [("bl2" if e else "blk", e, t) for e in (0, 1) for t in range(4)] + weights, 0.5, [], 66)
    for u in (0, 1):
        tasks["con", 0, u] = ([], [("lhs", 0)] + [("con", 0, 0)] * u, 0.6, [(("p", 0, u), ("near", 0), 131072)], 65)
        tasks["red", 0, u] = ([("p", 0, u)], [("con", 0, u)], 0.2, [], 70)
    return tasks


def schedule():
    tasks = tasks_of()
    free, arrival, done, order = {}, {}, set(), []
    now = 0.0
    while len(order) < len(tasks):
        ready, soonest = [], None
        for name, (needs, after, _, sends, rank) in tasks.items():
            if name in done or not all(a in done for a in after) or not all(m in arrival for m in needs):
                continue
            at = max([arrival[m] for m in needs], default=0.0)
            if name[0] == "start":
                at = max([at] + [sum(free.get(link, 0.0) for _, link, _ in sends) / len(sends) - BACKLOG])
            if at <= now:
                ready.append((rank, at, name))
            elif soonest is None or at < soonest:
                soonest = at
        if not ready:
            now = soonest
            continue
        name = min(ready, key=lambda r: r[:2])[2]
        needs, after, takes, sends, _ = tasks[name]
        now += takes
        for message, link, size in sends:
            links = [("x", 1), ("x", -1)] if link[0] == "xx" else [link]
            rate = NEAR_RATE if link[0] == "near" else RATE
            for way in links:
                free[way] = max(free.get(way, 0.0), now) + size / rate
            arrival[message] = max(free[way] for way in links) + (NEAR_LATENCY if link[0] == "near" else LATENCY)
        done.add(name)
        order.append(name)
    return order, now


ORDER = schedule()[0]


def kernel(l_ref, r_ref, w_ref, lm_ref, rm_ref, out_ref,
           L, R, W, lf, lp, acc, lhs, part, sib, away, far,
           g_send, g_recv, a_send, a_recv, r_send, r_recv, s_send, s_recv, o_send, o_recv):
    row, col = lax.axis_index("row"), lax.axis_index("col")
    x, core = row // 2, row % 2
    y, z = col // 4, col % 4
    sent = []

    def row_at(dx, e):
        other = core if e == 0 else 1 - core
        return ((x + dx + 4) % 4) * 2 + other

    def col_at(dy, dz):
        return ((y + dy + 4) % 4) * 4 + (z + dz + 4) % 4

    def put(src, dst, send, recv, device):
        copy = pltpu.make_async_remote_copy(
            src_ref=src, dst_ref=dst, send_sem=send, recv_sem=recv,
            device_id=device, device_id_type=MESH)
        copy.start()
        sent.append(copy)

    def arrived(dst, send, recv):
        pltpu.make_async_remote_copy(
            src_ref=dst, dst_ref=dst, send_sem=send, recv_sem=recv,
            device_id=(row_at(0, 1), col), device_id_type=MESH).wait_recv()

    barrier = pltpu.get_barrier_semaphore()
    peers = [(row, col_at(1, 0)), (row, col_at(-1, 0)), (row, col_at(0, 1)), (row, col_at(0, -1))]
    peers += [(row_at(dx, e), col) for dx in GROUPS for e in (0, 1) if (dx, e) != (0, 0)]
    for peer in peers:
        pl.semaphore_signal(barrier, inc=1, device_id=peer, device_id_type=MESH)

    for i in range(8):
        for t in range(2):
            keep = lm_ref[t, i].astype(F32)
            lf[t, i * 128:(i + 1) * 128, :] = l_ref[i * 128:(i + 1) * 128, t * 128:(t + 1) * 128].astype(F32) * keep
    for r in range(8):
        for t in range(2):
            for q in range(0, 16, 2):
                pair = [lf[t, pl.ds(8 * (q + s) + r, 8, stride=128), :] for s in (0, 1)]
                lp[r, q * 8:q * 8 + 16, t * 128:(t + 1) * 128] = jnp.concatenate(pair, axis=0).astype(BF16)
    own_l = pl.ds(pl.multiple_of(col * 256, 256), 256)
    own_w = pl.ds(pl.multiple_of(col * 128, 128), 128)
    row_w = pl.ds(pl.multiple_of(row * 128, 128), 128)
    L[0, :, own_l] = lp[row]

    pl.semaphore_wait(barrier, len(peers))

    def exchange_l(g, e):
        dx = GROUPS[g]
        slot = 2 * GROUPS.index(norm(-dx)) + e
        to = row_at(dx, e)
        put(lp.at[to], L.at[slot, :, own_l], a_send.at[0, 2 * g + e], a_recv.at[0, slot], (to, col))

    def exchange_w(g, e):
        dx = GROUPS[g]
        slot = 2 * GROUPS.index(norm(-dx)) + e
        to = row_at(dx, e)
        put(w_ref.at[pl.ds(pl.multiple_of(to * 128, 128), 128), :], W.at[own_w, row_w],
            a_send.at[1, 2 * g + e], a_recv.at[1, slot], (to, col))

    def exchanged_l(slot):
        arrived(L.at[slot, :, own_l], a_send.at[0, slot], a_recv.at[0, slot])

    def exchanged_w(slot):
        g, e = slot // 2, slot % 2
        lanes = pl.ds(pl.multiple_of(row_at(GROUPS[g], e) * 128, 128), 128)
        arrived(W.at[own_w, lanes], a_send.at[1, slot], a_recv.at[1, slot])

    def r_piece(dx, e, p):
        return R.at[pl.ds(pl.multiple_of(row_at(dx, e) * 512 + p * 128, 128), 128), :]

    r_count = [0]

    def r_put(dx, p, to):
        view = r_piece(dx, 0, p)
        if to is None:
            recv, device = s_recv.at[GROUPS.index(dx), p], (row_at(0, 1), col)
        else:
            recv, device = r_recv.at[GROUPS.index(norm(dx - to)), p], (row_at(to, 0), col)
        put(view, view, r_send.at[r_count[0]], recv, device)
        r_count[0] += 1

    def r_arrived(dx, p):
        arrived(r_piece(dx, 0, p), r_send.at[0], r_recv.at[GROUPS.index(dx), p])

    def r_start(p):
        here = pl.ds(pl.multiple_of(row * 512 + p * 128, 128), 128)
        for a in range(8):
            lanes = slice(a * 128, (a + 1) * 128)
            keep = rm_ref[p, a].astype(F32)
            R[here, lanes] = (r_ref[p * 128:(p + 1) * 128, lanes].astype(F32) * keep).astype(BF16)
        r_put(0, p, 1)
        r_put(0, p, -1)
        r_put(0, p, None)

    def r_got(d, p):
        r_arrived(d, p)
        if d != 2 and (p < 2) == (d == -1):
            r_put(d, p, -d)
        r_put(d, p, None)

    def r_all():
        for dx in GROUPS:
            for p in range(4):
                arrived(r_piece(dx, 1, p), s_send, s_recv.at[GROUPS.index(dx), p])

    def block(n, h, at):
        kind, g = ITEMS[n]
        lanes = pl.ds(pl.multiple_of(at * 256, 256), 256)
        if kind == "L":
            return L.at[2 * g + h, :, lanes]
        if kind == "S":
            return L.at[g, h * 64:(h + 1) * 64, lanes]
        return W.at[pl.ds(pl.multiple_of(at * 128 + (2 * g + h) * 32, 32), 32), :]

    def along(h, p, q):
        return col_at(p, q) if h == 0 else col_at(q, p)

    def sem_of(p, q):
        return 4 * (p % 4) + q % 4

    counts = {}

    def g_put(n, h, p, q, ep, eq):
        view = block(n, h, along(h, p, q))
        k = counts.get((n, h), 0)
        counts[n, h] = k + 1
        put(view, view, g_send.at[n, h, k], g_recv.at[n, h, sem_of(p - ep, q - eq)], (row, along(h, ep, eq)))

    def g_arrived(n, h, p, q):
        arrived(block(n, h, along(h, p, q)), g_send.at[n, h, 0], g_recv.at[n, h, sem_of(p, q)])

    def start(n, h):
        kind, g = ITEMS[n]
        if kind == "W" and (g, h) == (0, 0):
            W[own_w, row_w] = w_ref[row_w, :]
            for slot in range(1, 8):
                exchanged_w(slot)
        elif kind == "S" and g > 0 and h == 0:
            exchanged_l(g)
        elif kind == "L":
            exchanged_l(2 * g + h)
        for e in (1, -1):
            g_put(n, h, 0, 0, e, 0)
            g_put(n, h, 0, 0, 0, e)

    def got(n, h, p, q):
        g_arrived(n, h, p, q)
        way = 1 if n % 2 == 0 else -1
        if q == 0:
            if p == -way:
                g_put(n, h, p, 0, way, 0)
            for e in (1, -1):
                g_put(n, h, p, 0, 0, e)
        elif q == -1 and p in (0, 2):
            g_put(n, h, p, q, 0, 1)
        elif q == 1 and p in (-1, 1):
            g_put(n, h, p, q, 0, -1)

    def some(slots, lanes, offsets):
        total = None
        for dy, dz in offsets:
            at = pl.ds(pl.multiple_of(col_at(dy, dz) * 256, 256), 256)
            left = L[slots, :, at]
            term = jnp.dot(left.reshape(left.shape[0] * 128, 256), R[at, lanes], preferred_element_type=F32)
            total = term if total is None else total + term
        return total

    def multiply(g, t):
        lanes = slice(t * 256, (t + 1) * 256)
        if g == 3:
            acc[g, :, lanes] = some(slice(6, 8), lanes, NEAR)
        else:
            acc[g, :, lanes] = jnp.dot(L[2 * g:2 * g + 2].reshape(256, 4096), R[:, lanes], preferred_element_type=F32)

    def multiply_rest(g, t):
        lanes = slice(t * 256, (t + 1) * 256)
        acc[g, :, lanes] += some(slice(6, 8), lanes, FAR)

    def multiply_block(e, t):
        lanes = slice(t * 256, (t + 1) * 256)
        if e == 1:
            acc[0, 128:, lanes] = some(slice(1, 2), lanes, NEAR)
        else:
            acc[0, :128, lanes] = jnp.dot(L[0], R[:, lanes], preferred_element_type=F32)

    def multiply_block_rest(e, t):
        lanes = slice(t * 256, (t + 1) * 256)
        acc[0, 128:, lanes] += some(slice(1, 2), lanes, FAR)

    def left_of(g):
        for q in range(16):
            for a in range(8):
                both = [acc[g, e * 128 + q * 8:e * 128 + q * 8 + 8, a * 128:(a + 1) * 128] for e in (0, 1)]
                lhs[g, a * 16:(a + 1) * 16, q * 128:(q + 1) * 128] = jnp.concatenate(both, axis=0).astype(BF16)

    def contract(g, u):
        for t in (0, 1):
            lanes = slice(u * 512 + t * 256, u * 512 + (t + 1) * 256)
            share = jnp.dot(lhs[g], W[:, lanes], preferred_element_type=F32)
            part[g, u, :, :, :, t * 256:(t + 1) * 256] = share.reshape(8, 2, 8, 256)
        put(part.at[g, u, :, 1], sib.at[g, u], o_send.at[0, g, u], o_recv.at[0, g, u], (row_at(0, 1), col))

    def reduce(g, u):
        arrived(sib.at[g, u], o_send.at[0, g, u], o_recv.at[0, g, u])
        total = part[g, u, :, 0] + sib[g, u]
        if g == 0:
            part[g, u, :, 0] = total
        else:
            away[g - 1, u] = total.reshape(64, 512).astype(BF16)
            put(away.at[g - 1, u], far.at[g - 1, u], o_send.at[1, g, u], o_recv.at[1, g, u], (row_at(GROUPS[g], 0), col))

    def far_in(g, u):
        arrived(far.at[g - 1, u], o_send.at[1, g, u], o_recv.at[1, g, u])

    does = {
        "prep": lambda: None, "start": start, "got": got, "rstart": r_start, "rgot": r_got, "rall": r_all,
        "lswap": exchange_l, "wswap": exchange_w, "mul": multiply, "blk": multiply_block, "lhs": left_of, "con": contract,
        "add": multiply_rest, "bl2": multiply_block_rest, "red": reduce, "far": far_in,
    }
    for name, *which in ORDER:
        does[name](*which)
    for u in (0, 1):
        total = part[0, u, :, 0]
        for g in range(3):
            total = total + far[g, u].astype(F32).reshape(8, 8, 512)
        for a in range(8):
            out_ref[:, a, u * 512:(u + 1) * 512] = total[a]
    for copy in sent:
        copy.wait_send()


def body(left_tiles, right_tiles, left_mask, right_mask, cycle_weight):
    vmem = pl.BlockSpec(memory_space=pltpu.VMEM)
    smem = pl.BlockSpec(memory_space=pltpu.SMEM)
    dma = pltpu.SemaphoreType.DMA
    total = pl.pallas_call(
        kernel,
        out_shape=jax.ShapeDtypeStruct((8, 8, 1024), F32),
        in_specs=[vmem, vmem, vmem, smem, smem],
        out_specs=vmem,
        scratch_shapes=[
            pltpu.VMEM((8, 128, 4096), BF16),
            pltpu.VMEM((4096, 1024), BF16),
            pltpu.VMEM((2048, 1024), BF16),
            pltpu.VMEM((2, 1024, 128), F32),
            pltpu.VMEM((8, 128, 256), BF16),
            pltpu.VMEM((4, 256, 1024), F32),
            pltpu.VMEM((4, 128, 2048), BF16),
            pltpu.VMEM((4, 2, 8, 2, 8, 512), F32),
            pltpu.VMEM((4, 2, 8, 8, 512), F32),
            pltpu.VMEM((3, 2, 64, 512), BF16),
            pltpu.VMEM((3, 2, 64, 512), BF16),
            dma((len(ITEMS), 2, 15)),
            dma((len(ITEMS), 2, 16)),
            dma((2, 8)),
            dma((2, 8)),
            dma((28,)),
            dma((4, 4)),
            dma,
            dma((4, 4)),
            dma((2, 4, 2)),
            dma((2, 4, 2)),
        ],
        compiler_params=pltpu.CompilerParams(
            collective_id=0, has_side_effects=True, vmem_limit_bytes=56 * 1024 * 1024),
        cost_estimate=pl.CostEstimate(flops=11 * 10**9, bytes_accessed=4 * 2**20, transcendentals=0),
    )(left_tiles, right_tiles, cycle_weight, left_mask.T, right_mask)
    return total


def solution(mesh):
    placed = (P("row", "col"), P("row", "col"), P("row", "col"), P("row", "col"), P("col", "row"))
    return jax.shard_map(
        body, mesh=mesh, in_specs=placed, out_specs=P("row", "col", None), check_vma=False
    )
```

```python
import jax
import jax.numpy as jnp
from jax import lax
from jax.experimental import pallas as pl
from jax.experimental.pallas import tpu as pltpu
from jax.sharding import PartitionSpec as P

MESH = pl.DeviceIdType.MESH
F32 = jnp.float32
BF16 = jnp.bfloat16

GROUPS = (0, 2, -1, 1)
ITEMS = (("L", 0), ("L", 1), ("L", 2), ("L", 3), ("W", 0), ("W", 1))
RATE = 42000.0
NEAR_RATE = 300000.0
LATENCY = 2.5
NEAR_LATENCY = 1.0
BACKLOG = 8.0
DEPTH = 4


def norm(d):
    return (d + 1) % 4 - 1


LEAVES = tuple((p, 2) for p in (0, -1, 1, 2)) + ((0, 1), (2, 1), (-1, -1), (1, -1))


def opposite(h, p, q):
    return ("y" if (p != 0) == (h == 0) else "z", p + q)


def tasks_of():
    tasks = {}
    for n, (kind, g) in enumerate(ITEMS):
        size = 65536
        for h in (0, 1):
            way = 1 if n % 2 == 0 else -1

            def go(p, q, ep, eq):
                return (("g", n, h, norm(p - ep), norm(q - eq)), opposite(h, ep, eq), size)

            if kind == "W":
                needs = [("w", m) for m in range(1, 8)]
            else:
                needs = [("l", 2 * g + h)] if 2 * g + h else []
            sends = [go(0, 0, e, 0) for e in (1, -1)] + [go(0, 0, 0, e) for e in (1, -1)]
            before = [("start", n, 0)] if h else [("start", n - 1, 1)] if n else []
            if n >= DEPTH:
                needs = needs + [("g", n - DEPTH, m, 2, 2) for m in (0, 1)]
            tasks["start", n, h] = (needs, [("prep",)] + before, 0.15, sends, 5)
            for p in range(-1, 3):
                for q in range(-1, 3):
                    if (p, q) == (0, 0) or (p, q) in LEAVES:
                        continue
                    sends = []
                    if q == 0:
                        if p == -way:
                            sends.append(go(p, 0, way, 0))
                        sends += [go(p, 0, 0, e) for e in (1, -1)]
                    elif q == -1 and p in (0, 2):
                        sends.append(go(p, q, 0, 1))
                    elif q == 1 and p in (-1, 1):
                        sends.append(go(p, q, 0, -1))
                    tasks["got", n, h, p, q] = ([("g", n, h, p, q)], [("start", n, h)], 0.05 * (1 + len(sends)), sends, 10 + n)
    for p in range(4):
        sends = [(("r", -1, p), ("x", 1), 262144), (("r", 1, p), ("x", -1), 262144), (("s", 0, p), ("near", 0), 262144)]
        tasks["rstart", p] = ([], [("prep",)] + [("rstart", m) for m in range(p)], 0.5, sends, 40 + p)
        for d in (-1, 1):
            sends = [(("s", d, p), ("near", 0), 262144)]
            if (p < 2) == (d == -1):
                sends.append((("r", 2, p), ("x", -d), 262144))
            tasks["rgot", d, p] = ([("r", d, p)], [("rstart", p)], 0.1, sends, 20)
        tasks["rgot", 2, p] = ([("r", 2, p)], [("rstart", p)], 0.1, [(("s", 2, p), ("near", 0), 262144)], 20)
    tasks["rall",] = ([("s", d, p) for d in GROUPS for p in range(4)], [("rgot", d, p) for d in (-1, 1, 2) for p in range(4)], 0.1, [], 25)
    far = {-1: ("x", -1), 1: ("x", 1), 2: ("xx", 0)}
    for g in range(4):
        for e in (0, 1):
            slot = 2 * g + e
            if slot == 0:
                continue
            link = far.get(GROUPS[g], ("near", 0))
            tasks["lswap", g, e] = ([], [("prep",)], 0.05, [(("l", slot), link, 65536)], (30, 30, 40.5, 41.5)[g])
            tasks["wswap", g, e] = ([], [("prep",)], 0.05, [(("w", slot), link, 32768)], 42.5)
    tasks["prep",] = ([], [], 2.0, [], 0)

    def arrived(items, halves=(0, 1)):
        return [(k, n, h, p, q) for n in items for h in halves for p in range(-1, 3) for q in range(-1, 3)
                for k in ("got",) if (p, q) != (0, 0) and (p, q) not in LEAVES]

    def leaves(n, halves=(0, 1)):
        return [("g", n, h, p, q) for h in halves for p, q in LEAVES]

    for g in range(4):
        for t in range(4):
            tasks["mul", g, t] = (leaves(g), [("rall",)] + arrived((g,)) + [("mul", g, 0)] * (t > 0), 0.85, [], 60 + g)
    for u in range(4):
        product = [("mul", g, t) for g in range(4) for t in range(4)]
        tasks["con", u] = (leaves(4 + u // 2, (u % 2,)), product + arrived((4 + u // 2,), (u % 2,)), 0.8, [(("p", u), ("near", 0), 262144)], 55)
        tasks["red", u] = ([("p", u)], [("con", u)], 0.3, [(("f", u, g), far[GROUPS[g]], 32768) for g in (1, 2, 3)], 15)
        tasks["far", u] = ([("f", u, g) for g in (1, 2, 3)], [("red", u)], 0.3, [], 70)
    return tasks


def schedule():
    tasks = tasks_of()
    free, arrival, done, order = {}, {}, set(), []
    now = 0.0
    while len(order) < len(tasks):
        ready, soonest = [], None
        for name, (needs, after, _, sends, rank) in tasks.items():
            if name in done or not all(a in done for a in after) or not all(m in arrival for m in needs):
                continue
            at = max([arrival[m] for m in needs], default=0.0)
            if name[0] == "start":
                at = max([at] + [sum(free.get(link, 0.0) for _, link, _ in sends) / len(sends) - BACKLOG])
            if at <= now:
                ready.append((rank, at, name))
            elif soonest is None or at < soonest:
                soonest = at
        if not ready:
            now = soonest
            continue
        name = min(ready, key=lambda r: r[:2])[2]
        needs, after, takes, sends, _ = tasks[name]
        now += takes
        for message, link, size in sends:
            links = [("x", 1), ("x", -1)] if link[0] == "xx" else [link]
            rate = NEAR_RATE if link[0] == "near" else RATE
            for way in links:
                free[way] = max(free.get(way, 0.0), now) + size / rate
            arrival[message] = max(free[way] for way in links) + (NEAR_LATENCY if link[0] == "near" else LATENCY)
        done.add(name)
        order.append(name)
    return order, now


ORDER = schedule()[0]


def kernel(l_ref, r_ref, w_ref, lm_ref, rm_ref, out_ref,
           L, R, W, lf, lp, lhs, part, sib, away, far,
           g_send, g_recv, a_send, a_recv, r_send, r_recv, s_send, s_recv, o_send, o_recv):
    row, col = lax.axis_index("row"), lax.axis_index("col")
    x, core = row // 2, row % 2
    y, z = col // 4, col % 4
    sent = []

    def row_at(dx, e):
        other = core if e == 0 else 1 - core
        return ((x + dx + 4) % 4) * 2 + other

    def col_at(dy, dz):
        return ((y + dy + 4) % 4) * 4 + (z + dz + 4) % 4

    def put(src, dst, send, recv, device):
        copy = pltpu.make_async_remote_copy(
            src_ref=src, dst_ref=dst, send_sem=send, recv_sem=recv,
            device_id=device, device_id_type=MESH)
        copy.start()
        sent.append(copy)

    def arrived(dst, send, recv):
        pltpu.make_async_remote_copy(
            src_ref=dst, dst_ref=dst, send_sem=send, recv_sem=recv,
            device_id=(row_at(0, 1), col), device_id_type=MESH).wait_recv()

    barrier = pltpu.get_barrier_semaphore()
    peers = [(row, col_at(1, 0)), (row, col_at(-1, 0)), (row, col_at(0, 1)), (row, col_at(0, -1))]
    peers += [(row_at(dx, e), col) for dx in GROUPS for e in (0, 1) if (dx, e) != (0, 0)]
    for peer in peers:
        pl.semaphore_signal(barrier, inc=1, device_id=peer, device_id_type=MESH)

    for i in range(8):
        for t in range(2):
            keep = lm_ref[t, i].astype(F32)
            lf[t, i * 128:(i + 1) * 128, :] = l_ref[i * 128:(i + 1) * 128, t * 128:(t + 1) * 128].astype(F32) * keep
    for r in range(8):
        for t in range(2):
            for q in range(0, 16, 2):
                pair = [lf[t, pl.ds(8 * (q + s) + r, 8, stride=128), :] for s in (0, 1)]
                lp[r, q * 8:q * 8 + 16, t * 128:(t + 1) * 128] = jnp.concatenate(pair, axis=0).astype(BF16)
    own_l = pl.ds(pl.multiple_of(col * 256, 256), 256)
    own_w = pl.ds(pl.multiple_of(col * 128, 128), 128)
    row_w = pl.ds(pl.multiple_of(row * 128, 128), 128)
    L[0, :, own_l] = lp[row]

    pl.semaphore_wait(barrier, len(peers))

    def exchange_l(g, e):
        dx = GROUPS[g]
        slot = 2 * GROUPS.index(norm(-dx)) + e
        to = row_at(dx, e)
        put(lp.at[to], L.at[slot, :, own_l], a_send.at[0, 2 * g + e], a_recv.at[0, slot], (to, col))

    def exchange_w(g, e):
        dx = GROUPS[g]
        slot = 2 * GROUPS.index(norm(-dx)) + e
        to = row_at(dx, e)
        put(w_ref.at[pl.ds(pl.multiple_of(to * 128, 128), 128), :], W.at[own_w, row_w],
            a_send.at[1, 2 * g + e], a_recv.at[1, slot], (to, col))

    def exchanged_l(slot):
        arrived(L.at[slot, :, own_l], a_send.at[0, slot], a_recv.at[0, slot])

    def exchanged_w(slot):
        g, e = slot // 2, slot % 2
        lanes = pl.ds(pl.multiple_of(row_at(GROUPS[g], e) * 128, 128), 128)
        arrived(W.at[own_w, lanes], a_send.at[1, slot], a_recv.at[1, slot])

    def r_piece(dx, e, p):
        return R.at[pl.ds(pl.multiple_of(row_at(dx, e) * 512 + p * 128, 128), 128), :]

    r_count = [0]

    def r_put(dx, p, to):
        view = r_piece(dx, 0, p)
        if to is None:
            recv, device = s_recv.at[GROUPS.index(dx), p], (row_at(0, 1), col)
        else:
            recv, device = r_recv.at[GROUPS.index(norm(dx - to)), p], (row_at(to, 0), col)
        put(view, view, r_send.at[r_count[0]], recv, device)
        r_count[0] += 1

    def r_arrived(dx, p):
        arrived(r_piece(dx, 0, p), r_send.at[0], r_recv.at[GROUPS.index(dx), p])

    def r_start(p):
        here = pl.ds(pl.multiple_of(row * 512 + p * 128, 128), 128)
        for a in range(8):
            lanes = slice(a * 128, (a + 1) * 128)
            keep = rm_ref[p, a].astype(F32)
            R[here, lanes] = (r_ref[p * 128:(p + 1) * 128, lanes].astype(F32) * keep).astype(BF16)
        r_put(0, p, 1)
        r_put(0, p, -1)
        r_put(0, p, None)

    def r_got(d, p):
        r_arrived(d, p)
        if d != 2 and (p < 2) == (d == -1):
            r_put(d, p, -d)
        r_put(d, p, None)

    def r_all():
        for dx in GROUPS:
            for p in range(4):
                arrived(r_piece(dx, 1, p), s_send, s_recv.at[GROUPS.index(dx), p])

    def block(n, h, at):
        kind, g = ITEMS[n]
        if kind == "L":
            return L.at[2 * g + h, :, pl.ds(pl.multiple_of(at * 256, 256), 256)]
        u = 2 * g + h
        return W.at[pl.ds(pl.multiple_of(at * 128, 128), 128), u * 256:(u + 1) * 256]

    def along(h, p, q):
        return col_at(p, q) if h == 0 else col_at(q, p)

    def sem_of(p, q):
        return 4 * (p % 4) + q % 4

    counts = {}

    def g_put(n, h, p, q, ep, eq):
        view = block(n, h, along(h, p, q))
        k = counts.get((n, h), 0)
        counts[n, h] = k + 1
        put(view, view, g_send.at[n, h, k], g_recv.at[n, h, sem_of(p - ep, q - eq)], (row, along(h, ep, eq)))

    def g_arrived(n, h, p, q):
        arrived(block(n, h, along(h, p, q)), g_send.at[n, h, 0], g_recv.at[n, h, sem_of(p, q)])

    def start(n, h):
        kind, g = ITEMS[n]
        if kind == "W" and (g, h) == (0, 0):
            W[own_w, row_w] = w_ref[row_w, :]
            for slot in range(1, 8):
                exchanged_w(slot)
        elif kind == "L" and 2 * g + h > 0:
            exchanged_l(2 * g + h)
        for e in (1, -1):
            g_put(n, h, 0, 0, e, 0)
            g_put(n, h, 0, 0, 0, e)

    def got(n, h, p, q):
        g_arrived(n, h, p, q)
        way = 1 if n % 2 == 0 else -1
        if q == 0:
            if p == -way:
                g_put(n, h, p, 0, way, 0)
            for e in (1, -1):
                g_put(n, h, p, 0, 0, e)
        elif q == -1 and p in (0, 2):
            g_put(n, h, p, q, 0, 1)
        elif q == 1 and p in (-1, 1):
            g_put(n, h, p, q, 0, -1)

    def multiply(g, t):
        if t == 0:
            for h in (0, 1):
                for p, q in LEAVES:
                    g_arrived(g, h, p, q)
        total = jnp.dot(L[2 * g:2 * g + 2].reshape(256, 4096), R[:, t * 256:(t + 1) * 256], preferred_element_type=F32)
        for q in range(16):
            for s in (0, 1):
                both = [total[e * 128 + q * 8:e * 128 + q * 8 + 8, s * 128:(s + 1) * 128] for e in (0, 1)]
                row0 = g * 128 + (2 * t + s) * 16
                lhs[row0:row0 + 16, q * 128:(q + 1) * 128] = jnp.concatenate(both, axis=0).astype(BF16)

    def contract(u):
        for p, q in LEAVES:
            g_arrived(4 + u // 2, u % 2, p, q)
        share = jnp.dot(lhs[...], W[:, u * 256:(u + 1) * 256], preferred_element_type=F32)
        part[u] = share.reshape(4, 8, 2, 8, 256)
        put(part.at[u, :, :, 1], sib.at[u], o_send.at[u, 0], o_recv.at[u, 0], (row_at(0, 1), col))

    def reduce(u):
        arrived(sib.at[u], o_send.at[u, 0], o_recv.at[u, 0])
        for g in (1, 2, 3):
            away[g - 1, u] = (part[u, g, :, 0] + sib[u, g]).reshape(64, 256).astype(BF16)
            put(away.at[g - 1, u], far.at[g - 1, u], o_send.at[u, g], o_recv.at[u, g], (row_at(GROUPS[g], 0), col))

    def far_in(u):
        total = part[u, 0, :, 0] + sib[u, 0]
        for g in (1, 2, 3):
            arrived(far.at[g - 1, u], o_send.at[u, g], o_recv.at[u, g])
            total = total + far[g - 1, u].astype(F32).reshape(8, 8, 256)
        for a in range(8):
            out_ref[:, a, u * 256:(u + 1) * 256] = total[a]

    does = {
        "prep": lambda: None, "start": start, "got": got, "rstart": r_start, "rgot": r_got, "rall": r_all,
        "lswap": exchange_l, "wswap": exchange_w, "mul": multiply, "con": contract, "red": reduce, "far": far_in,
    }
    for name, *which in ORDER:
        does[name](*which)
    for copy in sent:
        copy.wait_send()


def body(left_tiles, right_tiles, left_mask, right_mask, cycle_weight):
    vmem = pl.BlockSpec(memory_space=pltpu.VMEM)
    smem = pl.BlockSpec(memory_space=pltpu.SMEM)
    dma = pltpu.SemaphoreType.DMA
    total = pl.pallas_call(
        kernel,
        out_shape=jax.ShapeDtypeStruct((8, 8, 1024), F32),
        in_specs=[vmem, vmem, vmem, smem, smem],
        out_specs=vmem,
        scratch_shapes=[
            pltpu.VMEM((8, 128, 4096), BF16),
            pltpu.VMEM((4096, 1024), BF16),
            pltpu.VMEM((2048, 1024), BF16),
            pltpu.VMEM((2, 1024, 128), F32),
            pltpu.VMEM((8, 128, 256), BF16),
            pltpu.VMEM((512, 2048), BF16),
            pltpu.VMEM((4, 4, 8, 2, 8, 256), F32),
            pltpu.VMEM((4, 4, 8, 8, 256), F32),
            pltpu.VMEM((3, 4, 64, 256), BF16),
            pltpu.VMEM((3, 4, 64, 256), BF16),
            dma((len(ITEMS), 2, 15)),
            dma((len(ITEMS), 2, 16)),
            dma((2, 8)),
            dma((2, 8)),
            dma((28,)),
            dma((4, 4)),
            dma,
            dma((4, 4)),
            dma((4, 4)),
            dma((4, 4)),
        ],
        compiler_params=pltpu.CompilerParams(
            collective_id=0, has_side_effects=True, vmem_limit_bytes=56 * 1024 * 1024),
        cost_estimate=pl.CostEstimate(flops=11 * 10**9, bytes_accessed=4 * 2**20, transcendentals=0),
    )(left_tiles, right_tiles, cycle_weight, left_mask.T, right_mask)
    return total


def solution(mesh):
    placed = (P("row", "col"), P("row", "col"), P("row", "col"), P("row", "col"), P("col", "row"))
    return jax.shard_map(
        body, mesh=mesh, in_specs=placed, out_specs=P("row", "col", None), check_vma=False
    )
```

```python
import jax
import jax.numpy as jnp
from jax import lax
from jax.experimental import pallas as pl
from jax.experimental.pallas import tpu as pltpu
from jax.sharding import PartitionSpec as P

MESH = pl.DeviceIdType.MESH
F32 = jnp.float32
BF16 = jnp.bfloat16

GROUPS = (0, 2, -1, 1)
ITEMS = (("L", 0), ("L", 1), ("L", 2), ("L", 3), ("W", 0), ("W", 1))
RATE = 43000.0
NEAR_RATE = 300000.0
LATENCY = 2.5
NEAR_LATENCY = 1.0
BACKLOG = 6.0
DEPTH = 4


def norm(d):
    return (d + 1) % 4 - 1


LEAVES = tuple((p, 2) for p in (0, -1, 1, 2)) + ((0, 1), (2, 1), (-1, -1), (1, -1))


def opposite(h, p, q):
    return ("y" if (p != 0) == (h == 0) else "z", p + q)


def tasks_of():
    tasks = {}
    for n, (kind, g) in enumerate(ITEMS):
        size = 65536
        for h in (0, 1):
            way = 1 if n % 2 == 0 else -1

            def go(p, q, ep, eq):
                return (("g", n, h, norm(p - ep), norm(q - eq)), opposite(h, ep, eq), size)

            if kind == "W":
                needs = [("w", m) for m in range(1, 8)]
            else:
                needs = [("l", 2 * g + h)] if 2 * g + h else []
            sends = [go(0, 0, e, 0) for e in (1, -1)] + [go(0, 0, 0, e) for e in (1, -1)]
            before = [("start", n, 0)] if h else [("start", n - 1, 1)] if n else []
            if n >= DEPTH:
                needs = needs + [("g", n - DEPTH, m, 2, 2) for m in (0, 1)]
            tasks["start", n, h] = (needs, [("prep",)] + before, 0.15, sends, 5)
            for p in range(-1, 3):
                for q in range(-1, 3):
                    if (p, q) == (0, 0) or (p, q) in LEAVES:
                        continue
                    sends = []
                    if q == 0:
                        if p == -way:
                            sends.append(go(p, 0, way, 0))
                        sends += [go(p, 0, 0, e) for e in (1, -1)]
                    elif q == -1 and p in (0, 2):
                        sends.append(go(p, q, 0, 1))
                    elif q == 1 and p in (-1, 1):
                        sends.append(go(p, q, 0, -1))
                    tasks["got", n, h, p, q] = ([("g", n, h, p, q)], [("start", n, h)], 0.05 * (1 + len(sends)), sends, 10 + n)
    for p in range(4):
        sends = [(("r", -1, p), ("x", 1), 262144), (("r", 1, p), ("x", -1), 262144), (("s", 0, p), ("near", 0), 262144)]
        tasks["rstart", p] = ([], [("prep",)] + [("rstart", m) for m in range(p)], 0.5, sends, 40 + p)
        for d in (-1, 1):
            sends = [(("s", d, p), ("near", 0), 262144)]
            if (p < 2) == (d == -1):
                sends.append((("r", 2, p), ("x", -d), 262144))
            tasks["rgot", d, p] = ([("r", d, p)], [("rstart", p)], 0.1, sends, 20)
        tasks["rgot", 2, p] = ([("r", 2, p)], [("rstart", p)], 0.1, [(("s", 2, p), ("near", 0), 262144)], 20)
    tasks["rall",] = ([("s", d, p) for d in GROUPS for p in range(4)], [("rgot", d, p) for d in (-1, 1, 2) for p in range(4)], 0.1, [], 25)
    far = {-1: ("x", -1), 1: ("x", 1), 2: ("xx", 0)}
    for g in range(4):
        for e in (0, 1):
            slot = 2 * g + e
            if slot == 0:
                continue
            link = far.get(GROUPS[g], ("near", 0))
            tasks["lswap", g, e] = ([], [("prep",)], 0.05, [(("l", slot), link, 65536)], (30, 30, 40.5, 41.5)[g])
            tasks["wswap", g, e] = ([], [("prep",)], 0.05, [(("w", slot), link, 32768)], 42.5)
    tasks["prep",] = ([], [], 2.0, [], 0)

    def arrived(items, halves=(0, 1)):
        return [(k, n, h, p, q) for n in items for h in halves for p in range(-1, 3) for q in range(-1, 3)
                for k in ("got",) if (p, q) != (0, 0) and (p, q) not in LEAVES]

    def leaves(n, halves=(0, 1)):
        return [("g", n, h, p, q) for h in halves for p, q in LEAVES]

    for g in range(4):
        for t in range(4):
            tasks["mul", g, t] = (leaves(g), [("rall",)] + arrived((g,)) + [("mul", g, 0)] * (t > 0), 0.85, [], 60 + g)
    for u in range(4):
        product = [("mul", g, t) for g in range(4) for t in range(4)]
        tasks["con", u] = (leaves(4 + u // 2, (u % 2,)), product + arrived((4 + u // 2,), (u % 2,)), 0.8, [(("p", u), ("near", 0), 262144)], 55)
        tasks["red", u] = ([("p", u)], [("con", u)], 0.3, [(("f", u, g), far[GROUPS[g]], 32768) for g in (1, 2, 3)], 15)
        tasks["far", u] = ([("f", u, g) for g in (1, 2, 3)], [("red", u)], 0.3, [], 70)
    return tasks


def schedule():
    tasks = tasks_of()
    free, arrival, done, order = {}, {}, set(), []
    now = 0.0
    while len(order) < len(tasks):
        ready, soonest = [], None
        for name, (needs, after, _, sends, rank) in tasks.items():
            if name in done or not all(a in done for a in after) or not all(m in arrival for m in needs):
                continue
            at = max([arrival[m] for m in needs], default=0.0)
            if name[0] == "start":
                at = max([at] + [sum(free.get(link, 0.0) for _, link, _ in sends) / len(sends) - BACKLOG])
            if at <= now:
                ready.append((rank, at, name))
            elif soonest is None or at < soonest:
                soonest = at
        if not ready:
            now = soonest
            continue
        name = min(ready, key=lambda r: r[:2])[2]
        needs, after, takes, sends, _ = tasks[name]
        now += takes
        for message, link, size in sends:
            links = [("x", 1), ("x", -1)] if link[0] == "xx" else [link]
            rate = NEAR_RATE if link[0] == "near" else RATE
            for way in links:
                free[way] = max(free.get(way, 0.0), now) + size / rate
            arrival[message] = max(free[way] for way in links) + (NEAR_LATENCY if link[0] == "near" else LATENCY)
        done.add(name)
        order.append(name)
    return order, now


ORDER = schedule()[0]


def kernel(l_ref, r_ref, w_ref, lm_ref, rm_ref, out_ref,
           L, R, W, lf, lp, lhs, part, sib, away, far,
           g_send, g_recv, a_send, a_recv, r_send, r_recv, s_send, s_recv, o_send, o_recv):
    row, col = lax.axis_index("row"), lax.axis_index("col")
    x, core = row // 2, row % 2
    y, z = col // 4, col % 4
    sent = []

    def row_at(dx, e):
        other = core if e == 0 else 1 - core
        return ((x + dx + 4) % 4) * 2 + other

    def col_at(dy, dz):
        return ((y + dy + 4) % 4) * 4 + (z + dz + 4) % 4

    def put(src, dst, send, recv, device):
        copy = pltpu.make_async_remote_copy(
            src_ref=src, dst_ref=dst, send_sem=send, recv_sem=recv,
            device_id=device, device_id_type=MESH)
        copy.start()
        sent.append(copy)

    def arrived(dst, send, recv):
        pltpu.make_async_remote_copy(
            src_ref=dst, dst_ref=dst, send_sem=send, recv_sem=recv,
            device_id=(row_at(0, 1), col), device_id_type=MESH).wait_recv()

    barrier = pltpu.get_barrier_semaphore()
    peers = [(row, col_at(1, 0)), (row, col_at(-1, 0)), (row, col_at(0, 1)), (row, col_at(0, -1))]
    peers += [(row_at(dx, e), col) for dx in GROUPS for e in (0, 1) if (dx, e) != (0, 0)]
    for peer in peers:
        pl.semaphore_signal(barrier, inc=1, device_id=peer, device_id_type=MESH)

    for i in range(8):
        for t in range(2):
            keep = lm_ref[t, i].astype(F32)
            lf[t, i * 128:(i + 1) * 128, :] = l_ref[i * 128:(i + 1) * 128, t * 128:(t + 1) * 128].astype(F32) * keep
    for r in range(8):
        for t in range(2):
            for q in range(0, 16, 2):
                pair = [lf[t, pl.ds(8 * (q + s) + r, 8, stride=128), :] for s in (0, 1)]
                lp[r, q * 8:q * 8 + 16, t * 128:(t + 1) * 128] = jnp.concatenate(pair, axis=0).astype(BF16)
    own_l = pl.ds(pl.multiple_of(col * 256, 256), 256)
    own_w = pl.ds(pl.multiple_of(col * 128, 128), 128)
    row_w = pl.ds(pl.multiple_of(row * 128, 128), 128)
    L[0, :, own_l] = lp[row]

    pl.semaphore_wait(barrier, len(peers))

    def exchange_l(g, e):
        dx = GROUPS[g]
        slot = 2 * GROUPS.index(norm(-dx)) + e
        to = row_at(dx, e)
        put(lp.at[to], L.at[slot, :, own_l], a_send.at[0, 2 * g + e], a_recv.at[0, slot], (to, col))

    def exchange_w(g, e):
        dx = GROUPS[g]
        slot = 2 * GROUPS.index(norm(-dx)) + e
        to = row_at(dx, e)
        put(w_ref.at[pl.ds(pl.multiple_of(to * 128, 128), 128), :], W.at[own_w, row_w],
            a_send.at[1, 2 * g + e], a_recv.at[1, slot], (to, col))

    def exchanged_l(slot):
        arrived(L.at[slot, :, own_l], a_send.at[0, slot], a_recv.at[0, slot])

    def exchanged_w(slot):
        g, e = slot // 2, slot % 2
        lanes = pl.ds(pl.multiple_of(row_at(GROUPS[g], e) * 128, 128), 128)
        arrived(W.at[own_w, lanes], a_send.at[1, slot], a_recv.at[1, slot])

    def r_piece(dx, e, p):
        return R.at[pl.ds(pl.multiple_of(row_at(dx, e) * 512 + p * 128, 128), 128), :]

    r_count = [0]

    def r_put(dx, p, to):
        view = r_piece(dx, 0, p)
        if to is None:
            recv, device = s_recv.at[GROUPS.index(dx), p], (row_at(0, 1), col)
        else:
            recv, device = r_recv.at[GROUPS.index(norm(dx - to)), p], (row_at(to, 0), col)
        put(view, view, r_send.at[r_count[0]], recv, device)
        r_count[0] += 1

    def r_arrived(dx, p):
        arrived(r_piece(dx, 0, p), r_send.at[0], r_recv.at[GROUPS.index(dx), p])

    def r_start(p):
        here = pl.ds(pl.multiple_of(row * 512 + p * 128, 128), 128)
        for a in range(8):
            lanes = slice(a * 128, (a + 1) * 128)
            keep = rm_ref[p, a].astype(F32)
            R[here, lanes] = (r_ref[p * 128:(p + 1) * 128, lanes].astype(F32) * keep).astype(BF16)
        r_put(0, p, 1)
        r_put(0, p, -1)
        r_put(0, p, None)

    def r_got(d, p):
        r_arrived(d, p)
        if d != 2 and (p < 2) == (d == -1):
            r_put(d, p, -d)
        r_put(d, p, None)

    def r_all():
        for dx in GROUPS:
            for p in range(4):
                arrived(r_piece(dx, 1, p), s_send, s_recv.at[GROUPS.index(dx), p])

    def block(n, h, at):
        kind, g = ITEMS[n]
        if kind == "L":
            return L.at[2 * g + h, :, pl.ds(pl.multiple_of(at * 256, 256), 256)]
        u = 2 * g + h
        return W.at[pl.ds(pl.multiple_of(at * 128, 128), 128), u * 256:(u + 1) * 256]

    def along(h, p, q):
        return col_at(p, q) if h == 0 else col_at(q, p)

    def sem_of(p, q):
        return 4 * (p % 4) + q % 4

    counts = {}

    def g_put(n, h, p, q, ep, eq):
        view = block(n, h, along(h, p, q))
        k = counts.get((n, h), 0)
        counts[n, h] = k + 1
        put(view, view, g_send.at[n, h, k], g_recv.at[n, h, sem_of(p - ep, q - eq)], (row, along(h, ep, eq)))

    def g_arrived(n, h, p, q):
        arrived(block(n, h, along(h, p, q)), g_send.at[n, h, 0], g_recv.at[n, h, sem_of(p, q)])

    def start(n, h):
        kind, g = ITEMS[n]
        if kind == "W" and (g, h) == (0, 0):
            W[own_w, row_w] = w_ref[row_w, :]
            for slot in range(1, 8):
                exchanged_w(slot)
        elif kind == "L" and 2 * g + h > 0:
            exchanged_l(2 * g + h)
        for e in (1, -1):
            g_put(n, h, 0, 0, e, 0)
            g_put(n, h, 0, 0, 0, e)

    def got(n, h, p, q):
        g_arrived(n, h, p, q)
        way = 1 if n % 2 == 0 else -1
        if q == 0:
            if p == -way:
                g_put(n, h, p, 0, way, 0)
            for e in (1, -1):
                g_put(n, h, p, 0, 0, e)
        elif q == -1 and p in (0, 2):
            g_put(n, h, p, q, 0, 1)
        elif q == 1 and p in (-1, 1):
            g_put(n, h, p, q, 0, -1)

    def multiply(g, t):
        if t == 0:
            for h in (0, 1):
                for p, q in LEAVES:
                    g_arrived(g, h, p, q)
        total = jnp.dot(L[2 * g:2 * g + 2].reshape(256, 4096), R[:, t * 256:(t + 1) * 256], preferred_element_type=F32)
        for q in range(16):
            for s in (0, 1):
                both = [total[e * 128 + q * 8:e * 128 + q * 8 + 8, s * 128:(s + 1) * 128] for e in (0, 1)]
                row0 = g * 128 + (2 * t + s) * 16
                lhs[row0:row0 + 16, q * 128:(q + 1) * 128] = jnp.concatenate(both, axis=0).astype(BF16)

    def contract(u):
        for p, q in LEAVES:
            g_arrived(4 + u // 2, u % 2, p, q)
        share = jnp.dot(lhs[...], W[:, u * 256:(u + 1) * 256], preferred_element_type=F32)
        part[u] = share.reshape(4, 8, 2, 8, 256)
        put(part.at[u, :, :, 1], sib.at[u], o_send.at[u, 0], o_recv.at[u, 0], (row_at(0, 1), col))

    def reduce(u):
        arrived(sib.at[u], o_send.at[u, 0], o_recv.at[u, 0])
        for g in (1, 2, 3):
            away[g - 1, u] = (part[u, g, :, 0] + sib[u, g]).reshape(64, 256).astype(BF16)
            put(away.at[g - 1, u], far.at[g - 1, u], o_send.at[u, g], o_recv.at[u, g], (row_at(GROUPS[g], 0), col))

    def far_in(u):
        total = part[u, 0, :, 0] + sib[u, 0]
        for g in (1, 2, 3):
            arrived(far.at[g - 1, u], o_send.at[u, g], o_recv.at[u, g])
            total = total + far[g - 1, u].astype(F32).reshape(8, 8, 256)
        for a in range(8):
            out_ref[:, a, u * 256:(u + 1) * 256] = total[a]

    does = {
        "prep": lambda: None, "start": start, "got": got, "rstart": r_start, "rgot": r_got, "rall": r_all,
        "lswap": exchange_l, "wswap": exchange_w, "mul": multiply, "con": contract, "red": reduce, "far": far_in,
    }
    for name, *which in ORDER:
        does[name](*which)
    for copy in sent:
        copy.wait_send()


def body(left_tiles, right_tiles, left_mask, right_mask, cycle_weight):
    vmem = pl.BlockSpec(memory_space=pltpu.VMEM)
    smem = pl.BlockSpec(memory_space=pltpu.SMEM)
    dma = pltpu.SemaphoreType.DMA
    total = pl.pallas_call(
        kernel,
        out_shape=jax.ShapeDtypeStruct((8, 8, 1024), F32),
        in_specs=[vmem, vmem, vmem, smem, smem],
        out_specs=vmem,
        scratch_shapes=[
            pltpu.VMEM((8, 128, 4096), BF16),
            pltpu.VMEM((4096, 1024), BF16),
            pltpu.VMEM((2048, 1024), BF16),
            pltpu.VMEM((2, 1024, 128), F32),
            pltpu.VMEM((8, 128, 256), BF16),
            pltpu.VMEM((512, 2048), BF16),
            pltpu.VMEM((4, 4, 8, 2, 8, 256), F32),
            pltpu.VMEM((4, 4, 8, 8, 256), F32),
            pltpu.VMEM((3, 4, 64, 256), BF16),
            pltpu.VMEM((3, 4, 64, 256), BF16),
            dma((len(ITEMS), 2, 15)),
            dma((len(ITEMS), 2, 16)),
            dma((2, 8)),
            dma((2, 8)),
            dma((28,)),
            dma((4, 4)),
            dma,
            dma((4, 4)),
            dma((4, 4)),
            dma((4, 4)),
        ],
        compiler_params=pltpu.CompilerParams(
            collective_id=0, has_side_effects=True, vmem_limit_bytes=56 * 1024 * 1024),
        cost_estimate=pl.CostEstimate(flops=11 * 10**9, bytes_accessed=4 * 2**20, transcendentals=0),
    )(left_tiles, right_tiles, cycle_weight, left_mask.T, right_mask)
    return total


def solution(mesh):
    placed = (P("row", "col"), P("row", "col"), P("row", "col"), P("row", "col"), P("col", "row"))
    return jax.shard_map(
        body, mesh=mesh, in_specs=placed, out_specs=P("row", "col", None), check_vma=False
    )
```

```python
import jax
import jax.numpy as jnp
from jax import lax
from jax.experimental import pallas as pl
from jax.experimental.pallas import tpu as pltpu
from jax.sharding import PartitionSpec as P

MESH = pl.DeviceIdType.MESH
F32 = jnp.float32
BF16 = jnp.bfloat16

GROUPS = (0, 2, -1, 1)
ITEMS = (("L", 0), ("L", 1), ("L", 2), ("L", 3), ("W", 0), ("W", 1))
RATE = 43000.0
NEAR_RATE = 300000.0
LATENCY = 2.5
NEAR_LATENCY = 1.0
BACKLOG = 5.0
DEPTH = 4


def norm(d):
    return (d + 1) % 4 - 1


LEAVES = tuple((p, 2) for p in (0, -1, 1, 2)) + ((0, 1), (2, 1), (-1, -1), (1, -1))


def opposite(h, p, q):
    return ("y" if (p != 0) == (h == 0) else "z", p + q)


def tasks_of():
    tasks = {}
    for n, (kind, g) in enumerate(ITEMS):
        size = 65536
        for h in (0, 1):
            way = 1 if n % 2 == 0 else -1

            def go(p, q, ep, eq):
                return (("g", n, h, norm(p - ep), norm(q - eq)), opposite(h, ep, eq), size)

            if kind == "W":
                needs = [("w", m) for m in range(1, 8)]
            else:
                needs = [("l", 2 * g + h)] if 2 * g + h else []
            sends = [go(0, 0, e, 0) for e in (1, -1)] + [go(0, 0, 0, e) for e in (1, -1)]
            before = [("start", n, 0)] if h else [("start", n - 1, 1)] if n else []
            if n >= DEPTH:
                needs = needs + [("g", n - DEPTH, m, 2, 2) for m in (0, 1)]
            tasks["start", n, h] = (needs, [("prep",)] + before, 0.15, sends, 5)
            for p in range(-1, 3):
                for q in range(-1, 3):
                    if (p, q) == (0, 0) or (p, q) in LEAVES:
                        continue
                    sends = []
                    if q == 0:
                        if p == -way:
                            sends.append(go(p, 0, way, 0))
                        sends += [go(p, 0, 0, e) for e in (1, -1)]
                    elif q == -1 and p in (0, 2):
                        sends.append(go(p, q, 0, 1))
                    elif q == 1 and p in (-1, 1):
                        sends.append(go(p, q, 0, -1))
                    tasks["got", n, h, p, q] = ([("g", n, h, p, q)], [("start", n, h)], 0.05 * (1 + len(sends)), sends, 10 + n)
    for p in range(4):
        sends = [(("r", -1, p), ("x", 1), 262144), (("r", 1, p), ("x", -1), 262144), (("s", 0, p), ("near", 0), 262144)]
        tasks["rstart", p] = ([], [("prep",)] + [("rstart", m) for m in range(p)], 0.5, sends, 40 + p)
        for d in (-1, 1):
            sends = [(("s", d, p), ("near", 0), 262144)]
            if (p < 2) == (d == -1):
                sends.append((("r", 2, p), ("x", -d), 262144))
            tasks["rgot", d, p] = ([("r", d, p)], [("rstart", p)], 0.1, sends, 20)
        tasks["rgot", 2, p] = ([("r", 2, p)], [("rstart", p)], 0.1, [(("s", 2, p), ("near", 0), 262144)], 20)
    tasks["rall",] = ([("s", d, p) for d in GROUPS for p in range(4)], [("rgot", d, p) for d in (-1, 1, 2) for p in range(4)], 0.1, [], 25)
    far = {-1: ("x", -1), 1: ("x", 1), 2: ("xx", 0)}
    for g in range(4):
        for e in (0, 1):
            slot = 2 * g + e
            if slot == 0:
                continue
            link = far.get(GROUPS[g], ("near", 0))
            tasks["lswap", g, e] = ([], [("prep",)], 0.05, [(("l", slot), link, 65536)], (30, 30, 40.5, 41.5)[g])
            tasks["wswap", g, e] = ([], [("prep",)], 0.05, [(("w", slot), link, 32768)], 42.5)
    tasks["prep",] = ([], [], 2.0, [], 0)

    def arrived(items, halves=(0, 1)):
        return [(k, n, h, p, q) for n in items for h in halves for p in range(-1, 3) for q in range(-1, 3)
                for k in ("got",) if (p, q) != (0, 0) and (p, q) not in LEAVES]

    def leaves(n, halves=(0, 1)):
        return [("g", n, h, p, q) for h in halves for p, q in LEAVES]

    for g in range(4):
        for t in range(4):
            tasks["mul", g, t] = (leaves(g), [("rall",)] + arrived((g,)) + [("mul", g, 0)] * (t > 0), 0.85, [], 60 + g)
    for u in range(4):
        product = [("mul", g, t) for g in range(4) for t in range(4)]
        tasks["con", u] = (leaves(4 + u // 2, (u % 2,)), product + arrived((4 + u // 2,), (u % 2,)), 0.8, [(("p", u), ("near", 0), 262144)], 55)
        tasks["red", u] = ([("p", u)], [("con", u)], 0.3, [(("f", u, g), far[GROUPS[g]], 32768) for g in (1, 2, 3)], 15)
        tasks["far", u] = ([("f", u, g) for g in (1, 2, 3)], [("red", u)], 0.3, [], 70)
    return tasks


def schedule():
    tasks = tasks_of()
    free, arrival, done, order = {}, {}, set(), []
    now = 0.0
    while len(order) < len(tasks):
        ready, soonest = [], None
        for name, (needs, after, _, sends, rank) in tasks.items():
            if name in done or not all(a in done for a in after) or not all(m in arrival for m in needs):
                continue
            at = max([arrival[m] for m in needs], default=0.0)
            if name[0] == "start":
                at = max([at] + [sum(free.get(link, 0.0) for _, link, _ in sends) / len(sends) - BACKLOG])
            if at <= now:
                ready.append((rank, at, name))
            elif soonest is None or at < soonest:
                soonest = at
        if not ready:
            now = soonest
            continue
        name = min(ready, key=lambda r: r[:2])[2]
        needs, after, takes, sends, _ = tasks[name]
        now += takes
        for message, link, size in sends:
            links = [("x", 1), ("x", -1)] if link[0] == "xx" else [link]
            rate = NEAR_RATE if link[0] == "near" else RATE
            for way in links:
                free[way] = max(free.get(way, 0.0), now) + size / rate
            arrival[message] = max(free[way] for way in links) + (NEAR_LATENCY if link[0] == "near" else LATENCY)
        done.add(name)
        order.append(name)
    return order, now


ORDER = schedule()[0]


def kernel(l_ref, r_ref, w_ref, lm_ref, rm_ref, out_ref,
           L, R, W, lf, lp, lhs, part, sib, away, far,
           g_send, g_recv, a_send, a_recv, r_send, r_recv, s_send, s_recv, o_send, o_recv):
    row, col = lax.axis_index("row"), lax.axis_index("col")
    x, core = row // 2, row % 2
    y, z = col // 4, col % 4
    sent = []

    def row_at(dx, e):
        other = core if e == 0 else 1 - core
        return ((x + dx + 4) % 4) * 2 + other

    def col_at(dy, dz):
        return ((y + dy + 4) % 4) * 4 + (z + dz + 4) % 4

    def put(src, dst, send, recv, device):
        copy = pltpu.make_async_remote_copy(
            src_ref=src, dst_ref=dst, send_sem=send, recv_sem=recv,
            device_id=device, device_id_type=MESH)
        copy.start()
        sent.append(copy)

    def arrived(dst, send, recv):
        pltpu.make_async_remote_copy(
            src_ref=dst, dst_ref=dst, send_sem=send, recv_sem=recv,
            device_id=(row_at(0, 1), col), device_id_type=MESH).wait_recv()

    barrier = pltpu.get_barrier_semaphore()
    peers = [(row, col_at(1, 0)), (row, col_at(-1, 0)), (row, col_at(0, 1)), (row, col_at(0, -1))]
    peers += [(row_at(dx, e), col) for dx in GROUPS for e in (0, 1) if (dx, e) != (0, 0)]
    for peer in peers:
        pl.semaphore_signal(barrier, inc=1, device_id=peer, device_id_type=MESH)

    for i in range(8):
        for t in range(2):
            keep = lm_ref[t, i].astype(F32)
            lf[t, i * 128:(i + 1) * 128, :] = l_ref[i * 128:(i + 1) * 128, t * 128:(t + 1) * 128].astype(F32) * keep
    for r in range(8):
        for t in range(2):
            for q in range(0, 16, 2):
                pair = [lf[t, pl.ds(8 * (q + s) + r, 8, stride=128), :] for s in (0, 1)]
                lp[r, q * 8:q * 8 + 16, t * 128:(t + 1) * 128] = jnp.concatenate(pair, axis=0).astype(BF16)
    own_l = pl.ds(pl.multiple_of(col * 256, 256), 256)
    own_w = pl.ds(pl.multiple_of(col * 128, 128), 128)
    row_w = pl.ds(pl.multiple_of(row * 128, 128), 128)
    L[0, :, own_l] = lp[row]

    pl.semaphore_wait(barrier, len(peers))

    def exchange_l(g, e):
        dx = GROUPS[g]
        slot = 2 * GROUPS.index(norm(-dx)) + e
        to = row_at(dx, e)
        put(lp.at[to], L.at[slot, :, own_l], a_send.at[0, 2 * g + e], a_recv.at[0, slot], (to, col))

    def exchange_w(g, e):
        dx = GROUPS[g]
        slot = 2 * GROUPS.index(norm(-dx)) + e
        to = row_at(dx, e)
        put(w_ref.at[pl.ds(pl.multiple_of(to * 128, 128), 128), :], W.at[own_w, row_w],
            a_send.at[1, 2 * g + e], a_recv.at[1, slot], (to, col))

    def exchanged_l(slot):
        arrived(L.at[slot, :, own_l], a_send.at[0, slot], a_recv.at[0, slot])

    def exchanged_w(slot):
        g, e = slot // 2, slot % 2
        lanes = pl.ds(pl.multiple_of(row_at(GROUPS[g], e) * 128, 128), 128)
        arrived(W.at[own_w, lanes], a_send.at[1, slot], a_recv.at[1, slot])

    def r_piece(dx, e, p):
        return R.at[pl.ds(pl.multiple_of(row_at(dx, e) * 512 + p * 128, 128), 128), :]

    r_count = [0]

    def r_put(dx, p, to):
        view = r_piece(dx, 0, p)
        if to is None:
            recv, device = s_recv.at[GROUPS.index(dx), p], (row_at(0, 1), col)
        else:
            recv, device = r_recv.at[GROUPS.index(norm(dx - to)), p], (row_at(to, 0), col)
        put(view, view, r_send.at[r_count[0]], recv, device)
        r_count[0] += 1

    def r_arrived(dx, p):
        arrived(r_piece(dx, 0, p), r_send.at[0], r_recv.at[GROUPS.index(dx), p])

    def r_start(p):
        here = pl.ds(pl.multiple_of(row * 512 + p * 128, 128), 128)
        for a in range(8):
            lanes = slice(a * 128, (a + 1) * 128)
            keep = rm_ref[p, a].astype(F32)
            R[here, lanes] = (r_ref[p * 128:(p + 1) * 128, lanes].astype(F32) * keep).astype(BF16)
        r_put(0, p, 1)
        r_put(0, p, -1)
        r_put(0, p, None)

    def r_got(d, p):
        r_arrived(d, p)
        if d != 2 and (p < 2) == (d == -1):
            r_put(d, p, -d)
        r_put(d, p, None)

    def r_all():
        for dx in GROUPS:
            for p in range(4):
                arrived(r_piece(dx, 1, p), s_send, s_recv.at[GROUPS.index(dx), p])

    def block(n, h, at):
        kind, g = ITEMS[n]
        if kind == "L":
            return L.at[2 * g + h, :, pl.ds(pl.multiple_of(at * 256, 256), 256)]
        u = 2 * g + h
        return W.at[pl.ds(pl.multiple_of(at * 128, 128), 128), u * 256:(u + 1) * 256]

    def along(h, p, q):
        return col_at(p, q) if h == 0 else col_at(q, p)

    def sem_of(p, q):
        return 4 * (p % 4) + q % 4

    counts = {}

    def g_put(n, h, p, q, ep, eq):
        view = block(n, h, along(h, p, q))
        k = counts.get((n, h), 0)
        counts[n, h] = k + 1
        put(view, view, g_send.at[n, h, k], g_recv.at[n, h, sem_of(p - ep, q - eq)], (row, along(h, ep, eq)))

    def g_arrived(n, h, p, q):
        arrived(block(n, h, along(h, p, q)), g_send.at[n, h, 0], g_recv.at[n, h, sem_of(p, q)])

    def start(n, h):
        kind, g = ITEMS[n]
        if kind == "W" and (g, h) == (0, 0):
            W[own_w, row_w] = w_ref[row_w, :]
            for slot in range(1, 8):
                exchanged_w(slot)
        elif kind == "L" and 2 * g + h > 0:
            exchanged_l(2 * g + h)
        for e in (1, -1):
            g_put(n, h, 0, 0, e, 0)
            g_put(n, h, 0, 0, 0, e)

    def got(n, h, p, q):
        g_arrived(n, h, p, q)
        way = 1 if n % 2 == 0 else -1
        if q == 0:
            if p == -way:
                g_put(n, h, p, 0, way, 0)
            for e in (1, -1):
                g_put(n, h, p, 0, 0, e)
        elif q == -1 and p in (0, 2):
            g_put(n, h, p, q, 0, 1)
        elif q == 1 and p in (-1, 1):
            g_put(n, h, p, q, 0, -1)

    def multiply(g, t):
        if t == 0:
            for h in (0, 1):
                for p, q in LEAVES:
                    g_arrived(g, h, p, q)
        total = jnp.dot(L[2 * g:2 * g + 2].reshape(256, 4096), R[:, t * 256:(t + 1) * 256], preferred_element_type=F32)
        for q in range(16):
            for s in (0, 1):
                both = [total[e * 128 + q * 8:e * 128 + q * 8 + 8, s * 128:(s + 1) * 128] for e in (0, 1)]
                row0 = g * 128 + (2 * t + s) * 16
                lhs[row0:row0 + 16, q * 128:(q + 1) * 128] = jnp.concatenate(both, axis=0).astype(BF16)

    def contract(u):
        for p, q in LEAVES:
            g_arrived(4 + u // 2, u % 2, p, q)
        share = jnp.dot(lhs[...], W[:, u * 256:(u + 1) * 256], preferred_element_type=F32)
        part[u] = share.reshape(4, 8, 2, 8, 256)
        put(part.at[u, :, :, 1], sib.at[u], o_send.at[u, 0], o_recv.at[u, 0], (row_at(0, 1), col))

    def reduce(u):
        arrived(sib.at[u], o_send.at[u, 0], o_recv.at[u, 0])
        for g in (1, 2, 3):
            away[g - 1, u] = (part[u, g, :, 0] + sib[u, g]).reshape(64, 256).astype(BF16)
            put(away.at[g - 1, u], far.at[g - 1, u], o_send.at[u, g], o_recv.at[u, g], (row_at(GROUPS[g], 0), col))

    def far_in(u):
        total = part[u, 0, :, 0] + sib[u, 0]
        for g in (1, 2, 3):
            arrived(far.at[g - 1, u], o_send.at[u, g], o_recv.at[u, g])
            total = total + far[g - 1, u].astype(F32).reshape(8, 8, 256)
        for a in range(8):
            out_ref[:, a, u * 256:(u + 1) * 256] = total[a]

    does = {
        "prep": lambda: None, "start": start, "got": got, "rstart": r_start, "rgot": r_got, "rall": r_all,
        "lswap": exchange_l, "wswap": exchange_w, "mul": multiply, "con": contract, "red": reduce, "far": far_in,
    }
    for name, *which in ORDER:
        does[name](*which)
    for copy in sent:
        copy.wait_send()


def body(left_tiles, right_tiles, left_mask, right_mask, cycle_weight):
    vmem = pl.BlockSpec(memory_space=pltpu.VMEM)
    smem = pl.BlockSpec(memory_space=pltpu.SMEM)
    dma = pltpu.SemaphoreType.DMA
    total = pl.pallas_call(
        kernel,
        out_shape=jax.ShapeDtypeStruct((8, 8, 1024), F32),
        in_specs=[vmem, vmem, vmem, smem, smem],
        out_specs=vmem,
        scratch_shapes=[
            pltpu.VMEM((8, 128, 4096), BF16),
            pltpu.VMEM((4096, 1024), BF16),
            pltpu.VMEM((2048, 1024), BF16),
            pltpu.VMEM((2, 1024, 128), F32),
            pltpu.VMEM((8, 128, 256), BF16),
            pltpu.VMEM((512, 2048), BF16),
            pltpu.VMEM((4, 4, 8, 2, 8, 256), F32),
            pltpu.VMEM((4, 4, 8, 8, 256), F32),
            pltpu.VMEM((3, 4, 64, 256), BF16),
            pltpu.VMEM((3, 4, 64, 256), BF16),
            dma((len(ITEMS), 2, 15)),
            dma((len(ITEMS), 2, 16)),
            dma((2, 8)),
            dma((2, 8)),
            dma((28,)),
            dma((4, 4)),
            dma,
            dma((4, 4)),
            dma((4, 4)),
            dma((4, 4)),
        ],
        compiler_params=pltpu.CompilerParams(
            collective_id=0, has_side_effects=True, vmem_limit_bytes=56 * 1024 * 1024),
        cost_estimate=pl.CostEstimate(flops=11 * 10**9, bytes_accessed=4 * 2**20, transcendentals=0),
    )(left_tiles, right_tiles, cycle_weight, left_mask.T, right_mask)
    return total


def solution(mesh):
    placed = (P("row", "col"), P("row", "col"), P("row", "col"), P("row", "col"), P("col", "row"))
    return jax.shard_map(
        body, mesh=mesh, in_specs=placed, out_specs=P("row", "col", None), check_vma=False
    )
```
